32 devices in a mesh: shot: 2 (over y), tx: 4 (over x, core), ty: 4 (over z).
Axes of the slice: x: 2, y: 2, z: 4, core: 2. Of those that a mesh axis runs over, the one named last changes fastest.
Arguments:
- wave_now: float32 [8, 64, 64, 128], P('shot', 'tx', 'ty'), may hold values from -6 to 6
- wave_prev: float32 [8, 64, 64, 128], P('shot', 'tx', 'ty'), may hold values from -6 to 6
- courant: float32 [64, 64, 128], P('tx', 'ty'), may hold values from 0.02 to 0.3
- rec_index: int32 [4, 4, 512], P('tx', 'ty'), may hold values from 0 to 32767
- rec_history: bfloat16 [8, 8, 4, 4, 512], P('shot', None, 'tx', 'ty'), may hold values from -6 to 6
- green: bfloat16 [2, 8192, 8192], P(None, ('tx', 'ty'), 'shot'), may hold values from -0.046875 to 0.046875
- lag_delay: int32 [2], replicated, may hold values from 1 to 8, as said below
- emit_cells: int32 [4, 4, 8, 512], P('tx', 'ty'), may hold values from 0 to 32767
- emit_weights: float32 [4, 4, 8, 512], P('tx', 'ty'), may hold values from 0.25 to 1
Outputs:
- wave_out: float32 [8, 64, 64, 128], P('shot', 'tx', 'ty')
- wave_last: float32 [8, 64, 64, 128], P('shot', 'tx', 'ty')
- emission: float32 [8, 8, 4, 4, 512], P('shot', None, 'tx', 'ty')
The draws below stay inside these ranges and needn't reach their ends.
Inputs may be any that keep to these rules, and one draw needn't show every extreme that they name: `lag_delay`: one lag group has delay 8, the other a smaller one.
All inputs are finite; a program needn't handle non-finite values.
Results may differ from the reference program's by a relative error of at most 0.0023.
Values may be sent and summed in bfloat16 or wider, within the bound.
A program may use at most 128 MiB of HBM per device.

```python
import math
import jax
import jax.numpy as jnp
from jax import lax

CX = 16
CY = 16
CZ = 128
STEPS = 8
HIST = 8
LAGS = 2
REC_TILE = 512
EMIT_TILE = 512
RECS = 8192
EMITS = 8192
SHOTS = 8
NX = 64
NY = 64
N_SHOT = 2
N_TX = 4
N_TY = 4


def draw_lag_delay(key, part):
    subkeys = jax.random.split(jax.random.fold_in(key, 11))
    other = jax.random.randint(subkeys[0], (), 1, HIST)
    flipped = jax.random.randint(subkeys[1], (), 0, 2)
    first = jnp.where(flipped == 0, HIST, other)
    second = jnp.where(flipped == 0, other, HIST)
    return jnp.stack([first, second]).astype(jnp.int32)


def plant(drawn, stream_key, low, high):
    spot = [jax.random.randint(jax.random.fold_in(stream_key, axis), (), 0, length) for axis, length in enumerate(drawn.shape)]
    widest = drawn.shape.index(max(drawn.shape))
    next_to = spot[:widest] + [(spot[widest] + 1) % drawn.shape[widest]] + spot[widest + 1:]
    return drawn.at[tuple(spot)].set(low).at[tuple(next_to)].set(high)


def block_levels(rng, shape, pieces, low, top_value):
    def one(position, parts):
        heights = jax.random.uniform(jax.random.fold_in(jax.random.fold_in(rng, 6), position), (parts,), jnp.float32, low / len(pieces), top_value / len(pieces))
        return jnp.repeat(jnp.exp(heights), shape[position] // parts).reshape((-1,) + (1,) * (len(shape) - position - 1))

    loudness = one(*pieces[0])
    for cut in pieces[1:]:
        loudness = loudness * one(*cut)
    return loudness


def noise(own_key, dims, spread, most, cuts=(), kind=jnp.bfloat16):
    entries = jax.random.normal(own_key, dims, jnp.float32) * spread
    if len(cuts) > 0:
        entries = block_levels(own_key, dims, cuts, -0.22, 0.18) * entries
    return jnp.clip(entries, min=-most, max=most).astype(kind)


def setup_inputs(seed: int = 0) -> dict:
    key_list = jax.random.split(jax.random.key(seed), 10)
    wave_now = noise(key_list[0], (SHOTS, NX, NY, CZ), 1.0, 6.0, ((0, 2), (1, 4), (2, 4)), jnp.float32)
    wave_prev = noise(key_list[1], (SHOTS, NX, NY, CZ), 1.0, 6.0, ((0, 2), (1, 4), (2, 4)), jnp.float32)
    courant = jnp.clip(jnp.exp(math.log(0.3) - 2.7080503 * jax.random.uniform(key_list[2], (NX, NY, CZ), jnp.float32) ** block_levels(key_list[2], (NX, NY, CZ), ((0, 4), (1, 4)), -0.2, 0.2)), 0.02, 0.3)
    rec_index = plant(jax.random.randint(key_list[3], (N_TX, N_TY, REC_TILE), 0, CX * CY * CZ), jax.random.fold_in(key_list[3], 1), 0, (CX * CY * CZ) - 1).astype(jnp.int32)
    rec_history = noise(key_list[4], (SHOTS, HIST, N_TX, N_TY, REC_TILE), 1.0, 6.0, ((0, 2), (2, 4), (3, 4)))
    green = noise(key_list[5], (LAGS, RECS, EMITS), (LAGS * RECS) ** -0.5, 0.046875, ((1, 16), (2, 2)))
    lag_delay = draw_lag_delay(jax.random.fold_in(key_list[9], 71), 0)
    emit_cells = plant(jax.random.randint(key_list[7], (N_TX, N_TY, 8, EMIT_TILE), 0, CX * CY * CZ), jax.random.fold_in(key_list[7], 1), 0, (CX * CY * CZ) - 1).astype(jnp.int32)
    emit_weights = jnp.clip(0.25 + 0.75 * jax.random.uniform(key_list[8], (N_TX, N_TY, 8, EMIT_TILE), jnp.float32) ** block_levels(key_list[8], (N_TX, N_TY, 8, EMIT_TILE), ((0, 4), (1, 4)), -0.2, 0.2), 0.25, 1.0)
    return {"wave_now": wave_now, "wave_prev": wave_prev, "courant": courant, "rec_index": rec_index, "rec_history": rec_history, "green": green, "lag_delay": lag_delay, "emit_cells": emit_cells, "emit_weights": emit_weights}


def laplace(field):
    padded = jnp.pad(field, ((0, 0), (1, 1), (1, 1), (1, 1)))
    centre = padded[:, 1:-1, 1:-1, 1:-1]
    total = padded[:, 2:, 1:-1, 1:-1] + padded[:, :-2, 1:-1, 1:-1]
    total = total + padded[:, 1:-1, 2:, 1:-1] + padded[:, 1:-1, :-2, 1:-1]
    total = total + padded[:, 1:-1, 1:-1, 2:] + padded[:, 1:-1, 1:-1, :-2]
    return total - 6.0 * centre


def tiles_view(field):
    shots_all = field.shape[0]
    viewed = field.reshape(shots_all, N_TX, CX, N_TY, CY, CZ).transpose(0, 1, 3, 2, 4, 5)
    return viewed.reshape(shots_all, N_TX, N_TY, CX * CY * CZ)


def reference(wave_now, wave_prev, courant, rec_index, rec_history, green, lag_delay, emit_cells, emit_weights):
    shots_all = wave_now.shape[0]
    current, previous = wave_now, wave_prev
    traces = []
    index_full = jnp.broadcast_to(rec_index[None], (shots_all,) + rec_index.shape)
    for step in range(STEPS):
        following = 2.0 * current - previous + courant[None] * laplace(current)
        previous, current = current, following
        sampled = jnp.take_along_axis(tiles_view(current), index_full, axis=3)
        traces.append(sampled.astype(jnp.bfloat16))
    new_records = jnp.stack(traces, 1)
    full = jnp.concatenate([rec_history, new_records], 1).reshape(shots_all, HIST + STEPS, RECS)
    columns = jnp.zeros((shots_all * STEPS, EMITS), jnp.float32)
    for lag_group in range(LAGS):
        offset = (HIST - lag_delay[lag_group]).astype(jnp.int32)
        window = lax.dynamic_slice_in_dim(full, offset, STEPS, 1).reshape(shots_all * STEPS, RECS)
        columns = columns + jnp.dot(window, green[lag_group], preferred_element_type=jnp.float32)
    columns = columns.reshape(shots_all, STEPS, N_SHOT, N_TX * N_TY, EMIT_TILE // N_SHOT)
    emission = columns.transpose(0, 1, 3, 2, 4).reshape(shots_all, STEPS, N_TX, N_TY, EMIT_TILE)
    last = emission[:, STEPS - 1]
    values = emit_weights[None] * last[:, :, :, None, :]
    shot_idx = jnp.arange(shots_all)[:, None, None, None, None]
    tile_a = jnp.arange(N_TX)[None, :, None, None, None]
    tile_b = jnp.arange(N_TY)[None, None, :, None, None]
    viewed = tiles_view(current).at[shot_idx, tile_a, tile_b, emit_cells[None]].add(values)
    wave_out = viewed.reshape(shots_all, N_TX, N_TY, CX, CY, CZ).transpose(0, 1, 3, 2, 4, 5)
    wave_out = wave_out.reshape(shots_all, N_TX * CX, N_TY * CY, CZ)
    return wave_out, previous, emission
```

```python
import functools

import jax
import jax.numpy as jnp
from jax import lax
from jax.experimental import pallas as pl
from jax.experimental.pallas import tpu as pltpu
from jax.sharding import PartitionSpec as P

STEPS = 8
HIST = 8
MIB = 1024 * 1024


def wave_kernel(
    n_tx, n_ty, now_ref, prev_ref, cour_ref, ridx_ref,
    last_ref, out_ref, rec_ref,
    field, ysend, yrecv, pick_xy, pick_z,
    load_sem, send_sem, recv_sem,
):
    shots, ext_x, ext_y, depth = now_ref.shape
    tx, ty = lax.axis_index("tx"), lax.axis_index("ty")
    there = (tx > 0, tx < n_tx - 1, ty > 0, ty < n_ty - 1)
    target = ({"tx": tx - 1}, {"tx": tx + 1}, {"ty": ty - 1}, {"ty": ty + 1})

    loads = [
        pltpu.make_async_copy(prev_ref, field.at[0, :, pl.ds(1, ext_x)], load_sem.at[0]),
        pltpu.make_async_copy(now_ref, field.at[1, :, pl.ds(1, ext_x)], load_sem.at[1]),
    ]
    for load in loads:
        load.start()

    barrier = pltpu.get_barrier_semaphore()
    for side in range(4):
        @pl.when(there[side])
        def _():
            pl.semaphore_signal(
                barrier, inc=1, device_id=target[side], device_id_type=pl.DeviceIdType.MESH
            )

    for side in range(4):
        @pl.when(jnp.logical_not(there[side]))
        def _():
            def clear(slot, carry):
                if side < 2:
                    field[slot, :, side * (ext_x + 1)] = jnp.zeros((shots, ext_y, depth), jnp.float32)
                else:
                    yrecv[slot, side - 2] = jnp.zeros((shots, ext_x, 1, depth), jnp.float32)
                return carry
            lax.fori_loop(1, STEPS + 1, clear, 0)

    cells = ridx_ref[...]
    points = cells.shape[1]
    rows = lax.broadcasted_iota(jnp.int32, (ext_x * ext_y, points), 0)
    pick_xy[...] = jnp.where(rows == cells // depth, 1.0, 0.0).astype(jnp.bfloat16)
    deep = lax.broadcasted_iota(jnp.int32, (depth, points), 0)
    pick_z[...] = jnp.where(deep == cells % depth, 1.0, 0.0)

    def copy(slot, side):
        if side < 2:
            src = field.at[slot, :, 1 if side == 0 else ext_x]
            dst = field.at[slot, :, ext_x + 1 if side == 0 else 0]
        else:
            src = ysend.at[slot, side - 2]
            dst = yrecv.at[slot, 3 - side]
        return pltpu.make_async_remote_copy(
            src_ref=src, dst_ref=dst,
            send_sem=send_sem.at[slot, side], recv_sem=recv_sem.at[slot, side ^ 1],
            device_id=target[side], device_id_type=pl.DeviceIdType.MESH,
        )

    def landing(slot, side):
        if side < 2:
            dst = field.at[slot, :, 0 if side == 0 else ext_x + 1]
        else:
            dst = yrecv.at[slot, side - 2]
        return pltpu.make_async_remote_copy(
            src_ref=dst, dst_ref=dst,
            send_sem=send_sem.at[slot, side], recv_sem=recv_sem.at[slot, side],
            device_id=target[side], device_id_type=pl.DeviceIdType.MESH,
        )

    def send(slot):
        for side in range(2):
            @pl.when(there[side])
            def _():
                copy(slot, side).start()
        ysend[slot, 0] = field[slot, :, 1 : ext_x + 1, 0:1, :]
        ysend[slot, 1] = field[slot, :, 1 : ext_x + 1, ext_y - 1 : ext_y, :]
        for side in range(2, 4):
            @pl.when(there[side])
            def _():
                copy(slot, side).start()

    for load in loads:
        load.wait()
    peers = sum(jnp.where(flag, 1, 0) for flag in there)
    pl.semaphore_wait(barrier, peers)
    send(1)

    part = 4 if ext_x % 4 == 0 else 1
    shape = (part, ext_y, depth)
    at_y = lax.broadcasted_iota(jnp.int32, shape, 1)
    at_z = lax.broadcasted_iota(jnp.int32, shape, 2)

    def advance(slot):
        def one_shot(s, carry):
            for x0 in range(0, ext_x, part):
                centre = field[slot, s, x0 + 1 : x0 + 1 + part]
                total = field[slot, s, x0 : x0 + part] + field[slot, s, x0 + 2 : x0 + 2 + part]
                low = jnp.broadcast_to(yrecv[slot, 0, s, x0 : x0 + part], shape)
                high = jnp.broadcast_to(yrecv[slot, 1, s, x0 : x0 + part], shape)
                total += jnp.where(at_y == 0, low, pltpu.roll(centre, 1, 1))
                total += jnp.where(at_y == ext_y - 1, high, pltpu.roll(centre, ext_y - 1, 1))
                total += jnp.where(at_z == 0, 0.0, pltpu.roll(centre, 1, 2))
                total += jnp.where(at_z == depth - 1, 0.0, pltpu.roll(centre, depth - 1, 2))
                before = field[slot - 1, s, x0 + 1 : x0 + 1 + part]
                speed = cour_ref[x0 : x0 + part]
                field[slot + 1, s, x0 + 1 : x0 + 1 + part] = (
                    2.0 * centre - before + speed * (total - 6.0 * centre)
                )
            return carry
        lax.fori_loop(0, shots, one_shot, 0)

    def sample(slot):
        for s in range(shots):
            tile = field[slot, s, 1 : ext_x + 1].reshape(ext_x * ext_y, depth).astype(jnp.bfloat16)
            found = lax.dot_general(
                tile, pick_xy[...], (((0,), (0,)), ((), ())), preferred_element_type=jnp.float32
            )
            rec_ref[slot - 2, s : s + 1, :] = jnp.sum(found * pick_z[...], axis=0, keepdims=True)

    def arrive(slot):
        for side in range(4):
            @pl.when(there[side])
            def _():
                landing(slot, side).wait_recv()

    def step(slot, carry):
        arrive(slot)
        advance(slot)
        send(slot + 1)
        sample(slot + 1)
        return carry

    lax.fori_loop(1, STEPS, step, 0)
    arrive(STEPS)
    advance(STEPS)
    sample(STEPS + 1)
    stores = [
        pltpu.make_async_copy(field.at[STEPS, :, pl.ds(1, ext_x)], last_ref, load_sem.at[0]),
        pltpu.make_async_copy(field.at[STEPS + 1, :, pl.ds(1, ext_x)], out_ref, load_sem.at[1]),
    ]
    for store in stores:
        store.start()

    def drain(slot, carry):
        for side in range(4):
            @pl.when(there[side])
            def _():
                copy(slot, side).wait_send()
        return carry
    lax.fori_loop(1, STEPS + 1, drain, 0)
    for store in stores:
        store.wait()


def run_wave(n_tx, n_ty, wave_now, wave_prev, courant, ridx):
    shots, ext_x, ext_y, depth = wave_now.shape
    points = ridx.shape[1]
    whole = pl.BlockSpec(memory_space=pltpu.VMEM)
    far = pl.BlockSpec(memory_space=pl.ANY)
    return pl.pallas_call(
        functools.partial(wave_kernel, n_tx, n_ty),
        out_shape=(
            jax.ShapeDtypeStruct(wave_now.shape, jnp.float32),
            jax.ShapeDtypeStruct(wave_now.shape, jnp.float32),
            jax.ShapeDtypeStruct((STEPS, shots, points), jnp.float32),
        ),
        in_specs=[far, far, whole, whole],
        out_specs=(far, far, whole),
        scratch_shapes=[
            pltpu.VMEM((STEPS + 2, shots, ext_x + 2, ext_y, depth), jnp.float32),
            pltpu.VMEM((STEPS + 1, 2, shots, ext_x, 1, depth), jnp.float32),
            pltpu.VMEM((STEPS + 1, 2, shots, ext_x, 1, depth), jnp.float32),
            pltpu.VMEM((ext_x * ext_y, points), jnp.bfloat16),
            pltpu.VMEM((depth, points), jnp.float32),
            pltpu.SemaphoreType.DMA((2,)),
            pltpu.SemaphoreType.DMA((STEPS + 1, 4)),
            pltpu.SemaphoreType.DMA((STEPS + 1, 4)),
        ],
        compiler_params=pltpu.CompilerParams(
            collective_id=0, has_side_effects=True, vmem_limit_bytes=40 * MIB
        ),
    )(wave_now, wave_prev, courant, ridx)


def inject_kernel(wave_ref, cells_ref, weights_ref, last_ref, out_ref):
    shots, ext_x, ext_y, depth = wave_ref.shape
    corners, points = cells_ref.shape
    rows = lax.broadcasted_iota(jnp.int32, (ext_x * ext_y, points), 0)
    deep = lax.broadcasted_iota(jnp.int32, (depth, points), 0)
    totals = [wave_ref[s].reshape(ext_x * ext_y, depth) for s in range(shots)]
    for k in range(corners):
        cells = cells_ref[k : k + 1, :]
        pick = jnp.where(rows == cells // depth, 1.0, 0.0).astype(jnp.bfloat16)
        here = deep == cells % depth
        values = weights_ref[k : k + 1, :] * last_ref[...]
        for s in range(shots):
            spread = jnp.where(here, values[s : s + 1, :], 0.0).astype(jnp.bfloat16)
            totals[s] += lax.dot_general(
                pick, spread, (((1,), (1,)), ((), ())), preferred_element_type=jnp.float32
            )
    for s in range(shots):
        out_ref[s] = totals[s].reshape(ext_x, ext_y, depth)


def inject(wave, cells, weights, last):
    whole = pl.BlockSpec(memory_space=pltpu.VMEM)
    return pl.pallas_call(
        inject_kernel,
        out_shape=jax.ShapeDtypeStruct(wave.shape, jnp.float32),
        in_specs=[whole] * 4,
        out_specs=whole,
        compiler_params=pltpu.CompilerParams(vmem_limit_bytes=40 * MIB),
    )(wave, cells, weights, last)


def local(
    n_tx, n_ty,
    wave_now, wave_prev, courant, rec_index, rec_history, green, lag_delay, emit_cells, emit_weights
):
    shots_here = wave_now.shape[0]
    previous, current, records = run_wave(
        n_tx, n_ty, wave_now, wave_prev, courant, rec_index.reshape(1, -1)
    )
    history_here = rec_history.reshape(shots_here, HIST, -1)
    new_here = records.astype(jnp.bfloat16).transpose(1, 0, 2)
    full_here = jnp.concatenate([history_here, new_here], 1)
    piece = lax.all_gather(full_here, "shot", axis=0, tiled=True)
    total = jnp.zeros((piece.shape[0], STEPS, green.shape[2]), jnp.float32)
    for lag_group in range(green.shape[0]):
        offset = HIST - lag_delay[lag_group]
        window = lax.dynamic_slice_in_dim(piece, offset, STEPS, 1)
        total = total + jnp.einsum(
            "str,rq->stq", window, green[lag_group], preferred_element_type=jnp.float32
        )
    summed = lax.psum_scatter(total, ("tx", "ty"), scatter_dimension=2, tiled=True)
    owned = lax.all_to_all(summed, "shot", split_axis=0, concat_axis=2, tiled=True)
    last = owned[:, STEPS - 1, :]
    wave_out = inject(
        current,
        emit_cells.reshape(emit_cells.shape[-2:]),
        emit_weights.reshape(emit_weights.shape[-2:]),
        last,
    )
    emission = owned.reshape(shots_here, STEPS, 1, 1, -1)
    return (wave_out, previous, emission)


def solution(mesh):
    return jax.shard_map(
        functools.partial(local, mesh.shape["tx"], mesh.shape["ty"]),
        mesh=mesh,
        in_specs=(
            P("shot", "tx", "ty", None),
            P("shot", "tx", "ty", None),
            P("tx", "ty", None),
            P("tx", "ty", None),
            P("shot", None, "tx", "ty", None),
            P(None, ("tx", "ty"), "shot"),
            P(),
            P("tx", "ty", None, None),
            P("tx", "ty", None, None),
        ),
        out_specs=(
            P("shot", "tx", "ty", None),
            P("shot", "tx", "ty", None),
            P("shot", None, "tx", "ty", None),
        ),
        check_vma=False,
    )
```

```python
import functools

import jax
import jax.numpy as jnp
from jax import lax
from jax.experimental import pallas as pl
from jax.experimental.pallas import tpu as pltpu
from jax.sharding import PartitionSpec as P

STEPS = 8
HIST = 8
MIB = 1024 * 1024


def flip(index, bit):
    return index + bit * (1 - 2 * ((index // bit) % 2))


def low_bit(m):
    return m & -m


def block_kernel(
    n_shot, n_tx, n_ty, lag_ref, now_ref, prev_ref, cour_ref, ridx_ref, hist_ref, green_ref,
    last_ref, out_ref, em_ref,
    field, ysend, yrecv, pick_xy, pick_z,
    hist_all, rec, rec_all, early, blocks, xpart, xrecv, zpart, zsend, zrecv,
    load_sem, send_sem, recv_sem, green_sem, hist_send, hist_recv, rec_send, rec_recv,
    x_send, x_recv, z_send, z_recv,
):
    mesh_id = pl.DeviceIdType.MESH
    shots, ext_x, ext_y, depth = now_ref.shape
    tx, ty = lax.axis_index("tx"), lax.axis_index("ty")
    me = lax.axis_index("shot")
    span = early.shape[2]
    each = span // n_ty
    rows_each = hist_ref.shape[0]
    group_a = jnp.where(lag_ref[0] == HIST, 0, 1)
    group_b = 1 - group_a
    short = jnp.where(lag_ref[0] == HIST, lag_ref[1], lag_ref[0])

    def green_tile(m):
        tile = tx
        bit = 1
        while bit < n_tx:
            if m & bit:
                tile = flip(tile, bit)
            bit *= 2
        return tile

    green_loads = []
    for group in range(green_ref.shape[0]):
        for m in range(n_tx):
            if span % 128 == 0:
                start = pl.multiple_of(green_tile(m) * span, span)
                src = green_ref.at[group, :, pl.ds(start, span)]
            else:
                src = green_ref.at[group, green_tile(m)]
            green_loads.append(
                pltpu.make_async_copy(src, blocks.at[group, m], green_sem.at[group, m])
            )
    there = (tx > 0, tx < n_tx - 1, ty > 0, ty < n_ty - 1)
    target = ({"tx": tx - 1}, {"tx": tx + 1}, {"ty": ty - 1}, {"ty": ty + 1})

    loads = [
        pltpu.make_async_copy(prev_ref, field.at[0, :, pl.ds(1, ext_x)], load_sem.at[0]),
        pltpu.make_async_copy(now_ref, field.at[1, :, pl.ds(1, ext_x)], load_sem.at[1]),
    ]
    for load in loads + green_loads:
        load.start()

    barrier = pltpu.get_barrier_semaphore()
    offsets = [
        (far, di) for far in range(n_ty) for di in range(n_shot) if far or di
    ]
    for step_x in range(1, n_tx):
        pl.semaphore_signal(
            barrier, inc=1, device_id={"tx": (tx + step_x) % n_tx}, device_id_type=mesh_id
        )

    def place(far, di):
        return (me + di) % n_shot, (ty + far) % n_ty

    for far, di in offsets:
        shot_to, ty_to = place(far, di)
        pl.semaphore_signal(
            barrier, inc=1, device_id={"shot": shot_to, "ty": ty_to}, device_id_type=mesh_id
        )

    def share(store, sends, recvs, di):
        return pltpu.make_async_remote_copy(
            src_ref=store.at[0], dst_ref=store.at[di],
            send_sem=sends.at[di], recv_sem=recvs.at[di],
            device_id={"shot": (me + di) % n_shot}, device_id_type=mesh_id,
        )

    hist_all[0] = hist_ref[...]
    rec[...] = jnp.zeros(rec.shape, jnp.float32)

    for side in range(4):
        @pl.when(jnp.logical_not(there[side]))
        def _():
            def clear(slot, carry):
                if side < 2:
                    field[slot, :, side * (ext_x + 1)] = jnp.zeros((shots, ext_y, depth), jnp.float32)
                else:
                    yrecv[slot, side - 2] = jnp.zeros((shots, ext_x, 1, depth), jnp.float32)
                return carry
            lax.fori_loop(1, STEPS + 1, clear, 0)

    cells = ridx_ref[...]
    points = cells.shape[1]
    rows = lax.broadcasted_iota(jnp.int32, (ext_x * ext_y, points), 0)
    pick_xy[...] = jnp.where(rows == cells // depth, 1.0, 0.0).astype(jnp.bfloat16)
    deep = lax.broadcasted_iota(jnp.int32, (depth, points), 0)
    pick_z[...] = jnp.where(deep == cells % depth, 1.0, 0.0)

    def copy(slot, side):
        if side < 2:
            src = field.at[slot, :, 1 if side == 0 else ext_x]
            dst = field.at[slot, :, ext_x + 1 if side == 0 else 0]
        else:
            src = ysend.at[slot, side - 2]
            dst = yrecv.at[slot, 3 - side]
        return pltpu.make_async_remote_copy(
            src_ref=src, dst_ref=dst,
            send_sem=send_sem.at[slot, side], recv_sem=recv_sem.at[slot, side ^ 1],
            device_id=target[side], device_id_type=pl.DeviceIdType.MESH,
        )

    def landing(slot, side):
        if side < 2:
            dst = field.at[slot, :, 0 if side == 0 else ext_x + 1]
        else:
            dst = yrecv.at[slot, side - 2]
        return pltpu.make_async_remote_copy(
            src_ref=dst, dst_ref=dst,
            send_sem=send_sem.at[slot, side], recv_sem=recv_sem.at[slot, side],
            device_id=target[side], device_id_type=pl.DeviceIdType.MESH,
        )

    def send(slot):
        for side in range(2):
            @pl.when(there[side])
            def _():
                copy(slot, side).start()
        ysend[slot, 0] = field[slot, :, 1 : ext_x + 1, 0:1, :]
        ysend[slot, 1] = field[slot, :, 1 : ext_x + 1, ext_y - 1 : ext_y, :]
        for side in range(2, 4):
            @pl.when(there[side])
            def _():
                copy(slot, side).start()

    for load in loads:
        load.wait()
    pl.semaphore_wait(barrier, n_tx - 1 + len(offsets))
    send(1)
    for di in range(1, n_shot):
        share(hist_all, hist_send, hist_recv, di).start()

    part = 4 if ext_x % 4 == 0 else 1
    shape = (part, ext_y, depth)
    at_y = lax.broadcasted_iota(jnp.int32, shape, 1)
    at_z = lax.broadcasted_iota(jnp.int32, shape, 2)

    def advance(slot):
        def one_shot(s, carry):
            for x0 in range(0, ext_x, part):
                centre = field[slot, s, x0 + 1 : x0 + 1 + part]
                total = field[slot, s, x0 : x0 + part] + field[slot, s, x0 + 2 : x0 + 2 + part]
                low = jnp.broadcast_to(yrecv[slot, 0, s, x0 : x0 + part], shape)
                high = jnp.broadcast_to(yrecv[slot, 1, s, x0 : x0 + part], shape)
                total += jnp.where(at_y == 0, low, pltpu.roll(centre, 1, 1))
                total += jnp.where(at_y == ext_y - 1, high, pltpu.roll(centre, ext_y - 1, 1))
                total += jnp.where(at_z == 0, 0.0, pltpu.roll(centre, 1, 2))
                total += jnp.where(at_z == depth - 1, 0.0, pltpu.roll(centre, depth - 1, 2))
                before = field[slot - 1, s, x0 + 1 : x0 + 1 + part]
                speed = cour_ref[x0 : x0 + part]
                field[slot + 1, s, x0 + 1 : x0 + 1 + part] = (
                    2.0 * centre - before + speed * (total - 6.0 * centre)
                )
            return carry
        lax.fori_loop(0, shots, one_shot, 0)

    def sample(slot):
        for s in range(shots):
            tile = field[slot, s, 1 : ext_x + 1].reshape(ext_x * ext_y, depth).astype(jnp.bfloat16)
            found = lax.dot_general(
                tile, pick_xy[...], (((0,), (0,)), ((), ())), preferred_element_type=jnp.float32
            )
            rec[pl.ds(s * STEPS + slot - 2, 1), :] = jnp.sum(
                found * pick_z[...], axis=0, keepdims=True
            )

    def arrive(slot):
        for side in range(4):
            @pl.when(there[side])
            def _():
                landing(slot, side).wait_recv()

    first_early = 2

    def early_part(m):
        early[m] = jnp.dot(
            hist_all[...].reshape(n_shot * rows_each, points), blocks[group_a, m],
            preferred_element_type=jnp.float32,
        )

    def step(slot, carry):
        arrive(slot)
        advance(slot)
        send(slot + 1)
        sample(slot + 1)

        @pl.when(slot == first_early)
        def _():
            for load in green_loads:
                load.wait()
            for di in range(1, n_shot):
                share(hist_all, hist_send, hist_recv, di).wait()

        @pl.when(jnp.logical_and(slot >= first_early, slot < first_early + n_tx))
        def _():
            early_part(slot - first_early)
        return carry

    lax.fori_loop(1, STEPS, step, 0)
    for m in range(STEPS - first_early, n_tx):
        early_part(m)

    rec_all[0] = rec[...].astype(jnp.bfloat16)
    for di in range(1, n_shot):
        share(rec_all, rec_send, rec_recv, di).start()
    arrive(STEPS)
    advance(STEPS)
    stores = [
        pltpu.make_async_copy(field.at[STEPS, :, pl.ds(1, ext_x)], last_ref, load_sem.at[0]),
        pltpu.make_async_copy(field.at[STEPS + 1, :, pl.ds(1, ext_x)], out_ref, load_sem.at[1]),
    ]
    for store in stores:
        store.start()
    for di in range(1, n_shot):
        share(rec_all, rec_send, rec_recv, di).wait()

    to_row = lax.broadcasted_iota(jnp.int32, (rows_each, rows_each), 0)
    of_row = lax.broadcasted_iota(jnp.int32, (rows_each, rows_each), 1)
    same = to_row // STEPS == of_row // STEPS
    wanted = to_row % STEPS - short
    pick_old = jnp.where(same & (of_row % STEPS == wanted + HIST), 1.0, 0.0).astype(jnp.bfloat16)
    pick_new = jnp.where(same & (of_row % STEPS == wanted), 1.0, 0.0).astype(jnp.bfloat16)
    windows = []
    for di in range(n_shot):
        window = jnp.dot(pick_old, hist_all[di], preferred_element_type=jnp.float32)
        window += jnp.dot(pick_new, rec_all[di], preferred_element_type=jnp.float32)
        windows.append(window.astype(jnp.bfloat16))
    window = jnp.concatenate(windows, 0)

    def hand_on(m):
        bit = low_bit(m)
        return pltpu.make_async_remote_copy(
            src_ref=xpart.at[m], dst_ref=xrecv.at[m],
            send_sem=x_send.at[m], recv_sem=x_recv.at[m],
            device_id={"tx": flip(tx, bit)}, device_id_type=mesh_id,
        )

    for m in range(n_tx - 1, -1, -1):
        part = early[m] + jnp.dot(window, blocks[group_b, m], preferred_element_type=jnp.float32)
        for di in range(n_shot):
            xpart[m, (me - di + n_shot) % n_shot] = part[di * rows_each : (di + 1) * rows_each]
        bit = 1
        while bit < (low_bit(m) if m else n_tx):
            hand_on(m + bit).wait_recv()
            xpart[m] += xrecv[m + bit]
            bit *= 2
        if m:
            hand_on(m).start()

    for b in range(n_ty):
        for i in range(n_shot):
            tile = xpart[0, i, :, b * each : (b + 1) * each]
            zpart[b, i] = tile
            zsend[b, i] = tile.astype(jnp.bfloat16)

    def deliver(far, di):
        shot_to, ty_to = place(far, di)
        return pltpu.make_async_remote_copy(
            src_ref=zsend.at[ty_to, shot_to], dst_ref=zrecv.at[far, di],
            send_sem=z_send.at[far, di], recv_sem=z_recv.at[far, di],
            device_id={"shot": shot_to, "ty": ty_to}, device_id_type=mesh_id,
        )

    for far, di in reversed(offsets):
        deliver(far, di).start()

    def drain(slot, carry):
        for side in range(4):
            @pl.when(there[side])
            def _():
                copy(slot, side).wait_send()
        return carry
    lax.fori_loop(1, STEPS + 1, drain, 0)
    for m in range(1, n_tx):
        hand_on(m).wait_send()

    for di in range(n_shot):
        if di == 0:
            total = zpart[ty, me]
        else:
            deliver(0, di).wait()
            total = zrecv[0, di].astype(jnp.float32)
        for far in range(1, n_ty):
            deliver(far, di).wait()
            total += zrecv[far, di].astype(jnp.float32)
        em_ref[(me - di + n_shot) % n_shot] = total
    for store in stores:
        store.wait()


def run_block(n_shot, n_tx, n_ty, lag_delay, wave_now, wave_prev, courant, ridx, history, green):
    shots, ext_x, ext_y, depth = wave_now.shape
    points = ridx.shape[1]
    groups = green.shape[0]
    rows_each = history.shape[0]
    span = green.shape[2] // n_tx
    each = span // n_ty
    if span % 128:
        green = green.reshape(groups, points, n_tx, span).transpose(0, 2, 1, 3)
    whole = pl.BlockSpec(memory_space=pltpu.VMEM)
    far = pl.BlockSpec(memory_space=pl.ANY)
    dma = pltpu.SemaphoreType.DMA
    return pl.pallas_call(
        functools.partial(block_kernel, n_shot, n_tx, n_ty),
        out_shape=(
            jax.ShapeDtypeStruct(wave_now.shape, jnp.float32),
            jax.ShapeDtypeStruct(wave_now.shape, jnp.float32),
            jax.ShapeDtypeStruct((n_shot, rows_each, each), jnp.float32),
        ),
        in_specs=[
            pl.BlockSpec(memory_space=pltpu.SMEM), far, far, whole, whole, whole, far
        ],
        out_specs=(far, far, whole),
        scratch_shapes=[
            pltpu.VMEM((STEPS + 2, shots, ext_x + 2, ext_y, depth), jnp.float32),
            pltpu.VMEM((STEPS + 1, 2, shots, ext_x, 1, depth), jnp.float32),
            pltpu.VMEM((STEPS + 1, 2, shots, ext_x, 1, depth), jnp.float32),
            pltpu.VMEM((ext_x * ext_y, points), jnp.bfloat16),
            pltpu.VMEM((depth, points), jnp.float32),
            pltpu.VMEM((n_shot, rows_each, points), jnp.bfloat16),
            pltpu.VMEM((rows_each, points), jnp.float32),
            pltpu.VMEM((n_shot, rows_each, points), jnp.bfloat16),
            pltpu.VMEM((n_tx, n_shot * rows_each, span), jnp.float32),
            pltpu.VMEM((groups, n_tx, points, span), jnp.bfloat16),
            pltpu.VMEM((n_tx, n_shot, rows_each, span), jnp.float32),
            pltpu.VMEM((n_tx, n_shot, rows_each, span), jnp.float32),
            pltpu.VMEM((n_ty, n_shot, rows_each, each), jnp.float32),
            pltpu.VMEM((n_ty, n_shot, rows_each, each), jnp.bfloat16),
            pltpu.VMEM((n_ty, n_shot, rows_each, each), jnp.bfloat16),
            dma((2,)),
            dma((STEPS + 1, 4)),
            dma((STEPS + 1, 4)),
            dma((groups, n_tx)),
            dma((n_shot,)),
            dma((n_shot,)),
            dma((n_shot,)),
            dma((n_shot,)),
            dma((n_tx,)),
            dma((n_tx,)),
            dma((n_ty, n_shot)),
            dma((n_ty, n_shot)),
        ],
        compiler_params=pltpu.CompilerParams(
            collective_id=0, has_side_effects=True, vmem_limit_bytes=52 * MIB
        ),
    )(lag_delay, wave_now, wave_prev, courant, ridx, history, green)


def inject_kernel(wave_ref, cells_ref, weights_ref, last_ref, out_ref):
    shots, ext_x, ext_y, depth = wave_ref.shape
    corners, points = cells_ref.shape
    rows = lax.broadcasted_iota(jnp.int32, (ext_x * ext_y, points), 0)
    deep = lax.broadcasted_iota(jnp.int32, (depth, points), 0)
    totals = [wave_ref[s].reshape(ext_x * ext_y, depth) for s in range(shots)]
    for k in range(corners):
        cells = cells_ref[k : k + 1, :]
        pick = jnp.where(rows == cells // depth, 1.0, 0.0).astype(jnp.bfloat16)
        here = deep == cells % depth
        values = weights_ref[k : k + 1, :] * last_ref[...]
        for s in range(shots):
            spread = jnp.where(here, values[s : s + 1, :], 0.0).astype(jnp.bfloat16)
            totals[s] += lax.dot_general(
                pick, spread, (((1,), (1,)), ((), ())), preferred_element_type=jnp.float32
            )
    for s in range(shots):
        out_ref[s] = totals[s].reshape(ext_x, ext_y, depth)


def inject(wave, cells, weights, last):
    whole = pl.BlockSpec(memory_space=pltpu.VMEM)
    return pl.pallas_call(
        inject_kernel,
        out_shape=jax.ShapeDtypeStruct(wave.shape, jnp.float32),
        in_specs=[whole] * 4,
        out_specs=whole,
        compiler_params=pltpu.CompilerParams(vmem_limit_bytes=40 * MIB),
    )(wave, cells, weights, last)


def local(
    n_shot, n_tx, n_ty,
    wave_now, wave_prev, courant, rec_index, rec_history, green, lag_delay, emit_cells, emit_weights
):
    shots_here = wave_now.shape[0]
    previous, current, columns = run_block(
        n_shot, n_tx, n_ty, lag_delay, wave_now, wave_prev, courant,
        rec_index.reshape(1, -1), rec_history.reshape(shots_here * HIST, -1), green,
    )
    owned = columns.reshape(n_shot, shots_here, STEPS, -1).transpose(1, 2, 0, 3)
    owned = owned.reshape(shots_here, STEPS, -1)
    wave_out = inject(
        current,
        emit_cells.reshape(emit_cells.shape[-2:]),
        emit_weights.reshape(emit_weights.shape[-2:]),
        owned[:, STEPS - 1, :],
    )
    return (wave_out, previous, owned.reshape(shots_here, STEPS, 1, 1, -1))


def solution(mesh):
    return jax.shard_map(
        functools.partial(local, mesh.shape["shot"], mesh.shape["tx"], mesh.shape["ty"]),
        mesh=mesh,
        in_specs=(
            P("shot", "tx", "ty", None),
            P("shot", "tx", "ty", None),
            P("tx", "ty", None),
            P("tx", "ty", None),
            P("shot", None, "tx", "ty", None),
            P(None, ("tx", "ty"), "shot"),
            P(),
            P("tx", "ty", None, None),
            P("tx", "ty", None, None),
        ),
        out_specs=(
            P("shot", "tx", "ty", None),
            P("shot", "tx", "ty", None),
            P("shot", None, "tx", "ty", None),
        ),
        check_vma=False,
    )
```

```python
import functools

import jax
import jax.numpy as jnp
from jax import lax
from jax.experimental import pallas as pl
from jax.experimental.pallas import tpu as pltpu
from jax.sharding import PartitionSpec as P

STEPS = 8
HIST = 8
MIB = 1024 * 1024


def flip(index, bit):
    return index + bit * (1 - 2 * ((index // bit) % 2))


def low_bit(m):
    return m & -m


def block_kernel(
    n_shot, n_tx, n_ty, lag_ref, now_ref, prev_ref, cour_far, ridx_far, hist_ref, green_ref,
    last_ref, out_ref, em_ref, cour_ref, ridx_ref,
    field, ysend, yrecv, pick_xy, pick_z,
    hist_all, rec, rec_all, early, blocks, xpart, xrecv, zpart, zsend, zrecv,
    load_sem, send_sem, recv_sem, green_sem, hist_send, hist_recv, rec_send, rec_recv,
    x_send, x_recv, z_send, z_recv,
):
    mesh_id = pl.DeviceIdType.MESH
    shots, ext_x, ext_y, depth = now_ref.shape
    tx, ty = lax.axis_index("tx"), lax.axis_index("ty")
    me = lax.axis_index("shot")
    span = early.shape[2]
    each = span // n_ty
    rows_each = hist_ref.shape[0]
    group_a = jnp.where(lag_ref[0] == HIST, 0, 1)
    group_b = 1 - group_a
    short = jnp.where(lag_ref[0] == HIST, lag_ref[1], lag_ref[0])

    def green_tile(m):
        tile = tx
        bit = 1
        while bit < n_tx:
            if m & bit:
                tile = flip(tile, bit)
            bit *= 2
        return tile

    green_loads = []
    for group in range(green_ref.shape[0]):
        for m in range(n_tx):
            if span % 128 == 0:
                start = pl.multiple_of(green_tile(m) * span, span)
                src = green_ref.at[group, :, pl.ds(start, span)]
            else:
                src = green_ref.at[group, green_tile(m)]
            green_loads.append(
                pltpu.make_async_copy(src, blocks.at[group, m], green_sem.at[group, m])
            )
    there = (tx > 0, tx < n_tx - 1, ty > 0, ty < n_ty - 1)
    target = ({"tx": tx - 1}, {"tx": tx + 1}, {"ty": ty - 1}, {"ty": ty + 1})

    loads = [
        pltpu.make_async_copy(prev_ref, field.at[0, :, pl.ds(1, ext_x)], load_sem.at[0]),
        pltpu.make_async_copy(now_ref, field.at[1, :, pl.ds(1, ext_x)], load_sem.at[1]),
        pltpu.make_async_copy(cour_far, cour_ref, load_sem.at[2]),
        pltpu.make_async_copy(ridx_far, ridx_ref, load_sem.at[3]),
        pltpu.make_async_copy(hist_ref, hist_all.at[0], load_sem.at[4]),
    ]
    for load in loads + green_loads:
        load.start()

    barrier = pltpu.get_barrier_semaphore()
    offsets = [
        (far, di) for far in range(n_ty) for di in range(n_shot) if far or di
    ]
    for step_x in range(1, n_tx):
        pl.semaphore_signal(
            barrier, inc=1, device_id={"tx": (tx + step_x) % n_tx}, device_id_type=mesh_id
        )

    def place(far, di):
        return (me + di) % n_shot, (ty + far) % n_ty

    for far, di in offsets:
        shot_to, ty_to = place(far, di)
        pl.semaphore_signal(
            barrier, inc=1, device_id={"shot": shot_to, "ty": ty_to}, device_id_type=mesh_id
        )

    def share(store, sends, recvs, di):
        return pltpu.make_async_remote_copy(
            src_ref=store.at[0], dst_ref=store.at[di],
            send_sem=sends.at[di], recv_sem=recvs.at[di],
            device_id={"shot": (me + di) % n_shot}, device_id_type=mesh_id,
        )

    rec[...] = jnp.zeros(rec.shape, jnp.float32)

    for side in range(4):
        @pl.when(jnp.logical_not(there[side]))
        def _():
            def clear(slot, carry):
                if side < 2:
                    field[slot, :, side * (ext_x + 1)] = jnp.zeros((shots, ext_y, depth), jnp.float32)
                else:
                    yrecv[slot, side - 2] = jnp.zeros((shots, ext_x, 1, depth), jnp.float32)
                return carry
            lax.fori_loop(1, STEPS + 1, clear, 0)

    def copy(slot, side):
        if side < 2:
            src = field.at[slot, :, 1 if side == 0 else ext_x]
            dst = field.at[slot, :, ext_x + 1 if side == 0 else 0]
        else:
            src = ysend.at[slot, side - 2]
            dst = yrecv.at[slot, 3 - side]
        return pltpu.make_async_remote_copy(
            src_ref=src, dst_ref=dst,
            send_sem=send_sem.at[slot, side], recv_sem=recv_sem.at[slot, side ^ 1],
            device_id=target[side], device_id_type=pl.DeviceIdType.MESH,
        )

    def landing(slot, side):
        if side < 2:
            dst = field.at[slot, :, 0 if side == 0 else ext_x + 1]
        else:
            dst = yrecv.at[slot, side - 2]
        return pltpu.make_async_remote_copy(
            src_ref=dst, dst_ref=dst,
            send_sem=send_sem.at[slot, side], recv_sem=recv_sem.at[slot, side],
            device_id=target[side], device_id_type=pl.DeviceIdType.MESH,
        )

    def send(slot):
        for side in (2, 3, 0, 1):
            @pl.when(there[side])
            def _():
                copy(slot, side).start()

    for load in loads[1:]:
        load.wait()
    ysend[1, 0] = field[1, :, 1 : ext_x + 1, 0:1, :]
    ysend[1, 1] = field[1, :, 1 : ext_x + 1, ext_y - 1 : ext_y, :]
    pl.semaphore_wait(barrier, n_tx - 1 + len(offsets))
    send(1)
    for di in range(1, n_shot):
        share(hist_all, hist_send, hist_recv, di).start()

    cells = ridx_ref[...]
    points = cells.shape[1]
    rows = lax.broadcasted_iota(jnp.int32, (ext_x * ext_y, points), 0)
    pick_xy[...] = jnp.where(rows == cells // depth, 1.0, 0.0).astype(jnp.bfloat16)
    deep = lax.broadcasted_iota(jnp.int32, (depth, points), 0)
    pick_z[...] = jnp.where(deep == cells % depth, 1.0, 0.0)

    loads[0].wait()

    part = 4 if ext_x % 4 == 0 else 1
    shape = (part, ext_y, depth)
    at_y = lax.broadcasted_iota(jnp.int32, shape, 1)
    at_z = lax.broadcasted_iota(jnp.int32, shape, 2)

    def inner(slot):
        def one_shot(s, carry):
            for x0 in range(0, ext_x, part):
                centre = field[slot, s, x0 + 1 : x0 + 1 + part]
                if x0 == 0:
                    below = [jnp.zeros((1, ext_y, depth), jnp.float32)]
                    if part > 1:
                        below.append(field[slot, s, 1:part])
                    below = jnp.concatenate(below, 0)
                else:
                    below = field[slot, s, x0 : x0 + part]
                if x0 + part == ext_x:
                    above = [jnp.zeros((1, ext_y, depth), jnp.float32)]
                    if part > 1:
                        above.insert(0, field[slot, s, x0 + 2 : ext_x + 1])
                    above = jnp.concatenate(above, 0)
                else:
                    above = field[slot, s, x0 + 2 : x0 + 2 + part]
                total = below + above
                total += jnp.where(at_y == 0, 0.0, pltpu.roll(centre, 1, 1))
                total += jnp.where(at_y == ext_y - 1, 0.0, pltpu.roll(centre, ext_y - 1, 1))
                total += jnp.where(at_z == 0, 0.0, pltpu.roll(centre, 1, 2))
                total += jnp.where(at_z == depth - 1, 0.0, pltpu.roll(centre, depth - 1, 2))
                before = field[slot - 1, s, x0 + 1 : x0 + 1 + part]
                speed = cour_ref[x0 : x0 + part]
                field[slot + 1, s, x0 + 1 : x0 + 1 + part] = (
                    2.0 * centre - before + speed * (total - 6.0 * centre)
                )
            return carry
        lax.fori_loop(0, shots, one_shot, 0)

    def border(slot, pack):
        for side in range(2):
            arrive(slot, side)
            halo, edge = (0, 1) if side == 0 else (ext_x + 1, ext_x)
            field[slot + 1, :, edge] += cour_ref[edge - 1][None] * field[slot, :, halo]
        for side in range(2, 4):
            arrive(slot, side)
            edge = 0 if side == 2 else ext_y - 1
            speed = cour_ref[:, edge : edge + 1, :]
            for s in range(shots):
                row = field[slot + 1, s, 1 : ext_x + 1, edge : edge + 1, :]
                row += speed * yrecv[slot, side - 2, s]
                if pack:
                    ysend[slot + 1, side - 2, s] = row
                field[slot + 1, s, 1 : ext_x + 1, edge : edge + 1, :] = row

    def sample(slot):
        for s in range(shots):
            tile = field[slot, s, 1 : ext_x + 1].reshape(ext_x * ext_y, depth).astype(jnp.bfloat16)
            found = lax.dot_general(
                tile, pick_xy[...], (((0,), (0,)), ((), ())), preferred_element_type=jnp.float32
            )
            rec[pl.ds(s * STEPS + slot - 2, 1), :] = jnp.sum(
                found * pick_z[...], axis=0, keepdims=True
            )

    def arrive(slot, side):
        @pl.when(there[side])
        def _():
            landing(slot, side).wait_recv()

    first_early = 2

    def early_part(m):
        early[m] = jnp.dot(
            hist_all[...].reshape(n_shot * rows_each, points), blocks[group_a, m],
            preferred_element_type=jnp.float32,
        )

    def step(slot, carry):
        border(slot, True)
        send(slot + 1)
        sample(slot + 1)
        inner(slot + 1)

        @pl.when(slot == first_early)
        def _():
            for load in green_loads:
                load.wait()
            for di in range(1, n_shot):
                share(hist_all, hist_send, hist_recv, di).wait()

        @pl.when(jnp.logical_and(slot >= first_early, slot < first_early + n_tx))
        def _():
            early_part(slot - first_early)
        return carry

    inner(1)
    lax.fori_loop(1, STEPS, step, 0)
    for m in range(STEPS - first_early, n_tx):
        early_part(m)

    rec_all[0] = rec[...].astype(jnp.bfloat16)
    for di in range(1, n_shot):
        share(rec_all, rec_send, rec_recv, di).start()
    border(STEPS, False)
    stores = [
        pltpu.make_async_copy(field.at[STEPS, :, pl.ds(1, ext_x)], last_ref, load_sem.at[0]),
        pltpu.make_async_copy(field.at[STEPS + 1, :, pl.ds(1, ext_x)], out_ref, load_sem.at[1]),
    ]
    for store in stores:
        store.start()
    for di in range(1, n_shot):
        share(rec_all, rec_send, rec_recv, di).wait()

    to_row = lax.broadcasted_iota(jnp.int32, (rows_each, rows_each), 0)
    of_row = lax.broadcasted_iota(jnp.int32, (rows_each, rows_each), 1)
    same = to_row // STEPS == of_row // STEPS
    wanted = to_row % STEPS - short
    pick_old = jnp.where(same & (of_row % STEPS == wanted + HIST), 1.0, 0.0).astype(jnp.bfloat16)
    pick_new = jnp.where(same & (of_row % STEPS == wanted), 1.0, 0.0).astype(jnp.bfloat16)
    windows = []
    for di in range(n_shot):
        window = jnp.dot(pick_old, hist_all[di], preferred_element_type=jnp.float32)
        window += jnp.dot(pick_new, rec_all[di], preferred_element_type=jnp.float32)
        windows.append(window.astype(jnp.bfloat16))
    window = jnp.concatenate(windows, 0)

    def hand_on(m):
        bit = low_bit(m)
        return pltpu.make_async_remote_copy(
            src_ref=xpart.at[m], dst_ref=xrecv.at[m],
            send_sem=x_send.at[m], recv_sem=x_recv.at[m],
            device_id={"tx": flip(tx, bit)}, device_id_type=mesh_id,
        )

    for m in range(n_tx - 1, -1, -1):
        part = early[m] + jnp.dot(window, blocks[group_b, m], preferred_element_type=jnp.float32)
        for di in range(n_shot):
            xpart[m, (me - di + n_shot) % n_shot] = part[di * rows_each : (di + 1) * rows_each]
        bit = 1
        while bit < (low_bit(m) if m else n_tx):
            hand_on(m + bit).wait_recv()
            xpart[m] += xrecv[m + bit]
            bit *= 2
        if m:
            hand_on(m).start()

    for b in range(n_ty):
        for i in range(n_shot):
            tile = xpart[0, i, :, b * each : (b + 1) * each]
            zpart[b, i] = tile
            zsend[b, i] = tile.astype(jnp.bfloat16)

    def deliver(far, di):
        shot_to, ty_to = place(far, di)
        return pltpu.make_async_remote_copy(
            src_ref=zsend.at[ty_to, shot_to], dst_ref=zrecv.at[far, di],
            send_sem=z_send.at[far, di], recv_sem=z_recv.at[far, di],
            device_id={"shot": shot_to, "ty": ty_to}, device_id_type=mesh_id,
        )

    for far, di in reversed(offsets):
        deliver(far, di).start()

    def drain(slot, carry):
        for side in range(4):
            @pl.when(there[side])
            def _():
                copy(slot, side).wait_send()
        return carry
    lax.fori_loop(1, STEPS + 1, drain, 0)
    for m in range(1, n_tx):
        hand_on(m).wait_send()

    for di in range(n_shot):
        if di == 0:
            total = zpart[ty, me]
        else:
            deliver(0, di).wait()
            total = zrecv[0, di].astype(jnp.float32)
        for far in range(1, n_ty):
            deliver(far, di).wait()
            total += zrecv[far, di].astype(jnp.float32)
        em_ref[(me - di + n_shot) % n_shot] = total
    for store in stores:
        store.wait()


def run_block(n_shot, n_tx, n_ty, lag_delay, wave_now, wave_prev, courant, ridx, history, green):
    shots, ext_x, ext_y, depth = wave_now.shape
    points = ridx.shape[1]
    groups = green.shape[0]
    rows_each = history.shape[0]
    span = green.shape[2] // n_tx
    each = span // n_ty
    if span % 128:
        green = green.reshape(groups, points, n_tx, span).transpose(0, 2, 1, 3)
    whole = pl.BlockSpec(memory_space=pltpu.VMEM)
    far = pl.BlockSpec(memory_space=pl.ANY)
    dma = pltpu.SemaphoreType.DMA
    return pl.pallas_call(
        functools.partial(block_kernel, n_shot, n_tx, n_ty),
        out_shape=(
            jax.ShapeDtypeStruct(wave_now.shape, jnp.float32),
            jax.ShapeDtypeStruct(wave_now.shape, jnp.float32),
            jax.ShapeDtypeStruct((n_shot, rows_each, each), jnp.float32),
        ),
        in_specs=[
            pl.BlockSpec(memory_space=pltpu.SMEM)
        ] + [pl.BlockSpec(memory_space=pltpu.HBM)] * 6,
        out_specs=(far, far, whole),
        scratch_shapes=[
            pltpu.VMEM((ext_x, ext_y, depth), jnp.float32),
            pltpu.VMEM((1, points), jnp.int32),
            pltpu.VMEM((STEPS + 2, shots, ext_x + 2, ext_y, depth), jnp.float32),
            pltpu.VMEM((STEPS + 1, 2, shots, ext_x, 1, depth), jnp.float32),
            pltpu.VMEM((STEPS + 1, 2, shots, ext_x, 1, depth), jnp.float32),
            pltpu.VMEM((ext_x * ext_y, points), jnp.bfloat16),
            pltpu.VMEM((depth, points), jnp.float32),
            pltpu.VMEM((n_shot, rows_each, points), jnp.bfloat16),
            pltpu.VMEM((rows_each, points), jnp.float32),
            pltpu.VMEM((n_shot, rows_each, points), jnp.bfloat16),
            pltpu.VMEM((n_tx, n_shot * rows_each, span), jnp.float32),
            pltpu.VMEM((groups, n_tx, points, span), jnp.bfloat16),
            pltpu.VMEM((n_tx, n_shot, rows_each, span), jnp.float32),
            pltpu.VMEM((n_tx, n_shot, rows_each, span), jnp.float32),
            pltpu.VMEM((n_ty, n_shot, rows_each, each), jnp.float32),
            pltpu.VMEM((n_ty, n_shot, rows_each, each), jnp.bfloat16),
            pltpu.VMEM((n_ty, n_shot, rows_each, each), jnp.bfloat16),
            dma((5,)),
            dma((STEPS + 1, 4)),
            dma((STEPS + 1, 4)),
            dma((groups, n_tx)),
            dma((n_shot,)),
            dma((n_shot,)),
            dma((n_shot,)),
            dma((n_shot,)),
            dma((n_tx,)),
            dma((n_tx,)),
            dma((n_ty, n_shot)),
            dma((n_ty, n_shot)),
        ],
        compiler_params=pltpu.CompilerParams(
            collective_id=0, has_side_effects=True, vmem_limit_bytes=52 * MIB
        ),
    )(lag_delay, wave_now, wave_prev, courant, ridx, history, green)


def inject_kernel(
    previous_ref, wave_ref, cells_ref, weights_ref, columns_ref,
    out_ref, last_ref, emission_ref, done, sems,
):
    shots, ext_x, ext_y, depth = wave_ref.shape
    n_shot, rows_each, each = columns_ref.shape
    corners = cells_ref.shape[0]
    keep = pltpu.make_async_copy(previous_ref, last_ref, sems.at[shots])
    keep.start()
    for s in range(shots):
        for t in range(STEPS):
            for i in range(n_shot):
                emission_ref[s, t, 0, :, i * each : (i + 1) * each] = columns_ref[
                    i, s * STEPS + t : s * STEPS + t + 1, :
                ]
    rows = lax.broadcasted_iota(jnp.int32, (ext_x * ext_y, each), 0)
    deep = lax.broadcasted_iota(jnp.int32, (depth, each), 0)
    totals = [wave_ref[s].reshape(ext_x * ext_y, depth) for s in range(shots)]
    for k in range(corners):
        for i in range(n_shot):
            span = slice(i * each, (i + 1) * each)
            cells = cells_ref[k : k + 1, span]
            pick = jnp.where(rows == cells // depth, 1.0, 0.0).astype(jnp.bfloat16)
            here = deep == cells % depth
            for s in range(shots):
                final = (s + 1) * STEPS - 1
                values = weights_ref[k : k + 1, span] * columns_ref[i, final : final + 1, :]
                spread = jnp.where(here, values, 0.0).astype(jnp.bfloat16)
                totals[s] += lax.dot_general(
                    pick, spread, (((1,), (1,)), ((), ())), preferred_element_type=jnp.float32
                )
    stores = []
    for s in range(shots):
        done[s] = totals[s].reshape(ext_x, ext_y, depth)
        stores.append(pltpu.make_async_copy(done.at[s], out_ref.at[s], sems.at[s]))
        stores[-1].start()
    for store in stores + [keep]:
        store.wait()


def inject(previous, wave, cells, weights, columns):
    whole = pl.BlockSpec(memory_space=pltpu.VMEM)
    far = pl.BlockSpec(memory_space=pl.ANY)
    shots = wave.shape[0]
    points = cells.shape[1]
    return pl.pallas_call(
        inject_kernel,
        out_shape=(
            jax.ShapeDtypeStruct(wave.shape, jnp.float32),
            jax.ShapeDtypeStruct(wave.shape, jnp.float32),
            jax.ShapeDtypeStruct((shots, STEPS, 1, 1, points), jnp.float32),
        ),
        in_specs=[far] + [whole] * 4,
        out_specs=(far, far, whole),
        scratch_shapes=[
            pltpu.VMEM(wave.shape, jnp.float32),
            pltpu.SemaphoreType.DMA((shots + 1,)),
        ],
        compiler_params=pltpu.CompilerParams(vmem_limit_bytes=40 * MIB),
    )(previous, wave, cells, weights, columns)


def local(
    n_shot, n_tx, n_ty,
    wave_now, wave_prev, courant, rec_index, rec_history, green, lag_delay, emit_cells, emit_weights
):
    shots_here = wave_now.shape[0]
    previous, current, columns = run_block(
        n_shot, n_tx, n_ty, lag_delay, wave_now, wave_prev, courant,
        rec_index.reshape(1, -1), rec_history.reshape(shots_here * HIST, -1), green,
    )
    return inject(
        previous,
        current,
        emit_cells.reshape(emit_cells.shape[-2:]),
        emit_weights.reshape(emit_weights.shape[-2:]),
        columns,
    )


def solution(mesh):
    return jax.shard_map(
        functools.partial(local, mesh.shape["shot"], mesh.shape["tx"], mesh.shape["ty"]),
        mesh=mesh,
        in_specs=(
            P("shot", "tx", "ty", None),
            P("shot", "tx", "ty", None),
            P("tx", "ty", None),
            P("tx", "ty", None),
            P("shot", None, "tx", "ty", None),
            P(None, ("tx", "ty"), "shot"),
            P(),
            P("tx", "ty", None, None),
            P("tx", "ty", None, None),
        ),
        out_specs=(
            P("shot", "tx", "ty", None),
            P("shot", "tx", "ty", None),
            P("shot", None, "tx", "ty", None),
        ),
        check_vma=False,
    )
```

```python
import functools

import jax
import jax.numpy as jnp
from jax import lax
from jax.experimental import pallas as pl
from jax.experimental.pallas import tpu as pltpu
from jax.sharding import PartitionSpec as P

STEPS = 8
HIST = 8
MIB = 1024 * 1024


def flip(index, bit):
    return index + bit * (1 - 2 * ((index // bit) % 2))


def low_bit(m):
    return m & -m


def block_kernel(
    n_shot, n_tx, n_ty, lag_ref, now_ref, prev_ref, cour_far, ridx_far, hist_ref, green_ref,
    last_ref, out_ref, em_ref, cour_ref, ridx_ref,
    field, ysend, yrecv, pick_xy, pick_z,
    hist_all, rec, rec_all, early, blocks, xpart, xrecv, zpart, zsend, zrecv,
    load_sem, send_sem, recv_sem, green_sem, hist_send, hist_recv, rec_send, rec_recv,
    x_send, x_recv, z_send, z_recv,
):
    mesh_id = pl.DeviceIdType.MESH
    shots, ext_x, ext_y, depth = now_ref.shape
    tx, ty = lax.axis_index("tx"), lax.axis_index("ty")
    me = lax.axis_index("shot")
    span = early.shape[2]
    each = span // n_ty
    rows_each = hist_ref.shape[0]
    group_a = jnp.where(lag_ref[0] == HIST, 0, 1)
    group_b = 1 - group_a
    short = jnp.where(lag_ref[0] == HIST, lag_ref[1], lag_ref[0])

    def green_tile(m):
        tile = tx
        bit = 1
        while bit < n_tx:
            if m & bit:
                tile = flip(tile, bit)
            bit *= 2
        return tile

    green_loads = []
    for group in range(green_ref.shape[0]):
        for m in range(n_tx):
            if span % 128 == 0:
                start = pl.multiple_of(green_tile(m) * span, span)
                src = green_ref.at[group, :, pl.ds(start, span)]
            else:
                src = green_ref.at[group, green_tile(m)]
            green_loads.append(
                pltpu.make_async_copy(src, blocks.at[group, m], green_sem.at[group, m])
            )
    there = (tx > 0, tx < n_tx - 1, ty > 0, ty < n_ty - 1)
    target = ({"tx": tx - 1}, {"tx": tx + 1}, {"ty": ty - 1}, {"ty": ty + 1})

    loads = [
        pltpu.make_async_copy(prev_ref, field.at[0, :, pl.ds(1, ext_x)], load_sem.at[0]),
        pltpu.make_async_copy(now_ref, field.at[1, :, pl.ds(1, ext_x)], load_sem.at[1]),
        pltpu.make_async_copy(cour_far, cour_ref, load_sem.at[2]),
        pltpu.make_async_copy(ridx_far, ridx_ref, load_sem.at[3]),
        pltpu.make_async_copy(hist_ref, hist_all.at[0], load_sem.at[4]),
    ]
    for load in loads + green_loads:
        load.start()

    barrier = pltpu.get_barrier_semaphore()
    offsets = [
        (far, di) for far in range(n_ty) for di in range(n_shot) if far or di
    ]
    for step_x in range(1, n_tx):
        pl.semaphore_signal(
            barrier, inc=1, device_id={"tx": (tx + step_x) % n_tx}, device_id_type=mesh_id
        )

    def place(far, di):
        return (me + di) % n_shot, (ty + far) % n_ty

    for far, di in offsets:
        shot_to, ty_to = place(far, di)
        pl.semaphore_signal(
            barrier, inc=1, device_id={"shot": shot_to, "ty": ty_to}, device_id_type=mesh_id
        )

    def share(store, sends, recvs, di):
        return pltpu.make_async_remote_copy(
            src_ref=store.at[0], dst_ref=store.at[di],
            send_sem=sends.at[di], recv_sem=recvs.at[di],
            device_id={"shot": (me + di) % n_shot}, device_id_type=mesh_id,
        )

    rec[...] = jnp.zeros(rec.shape, jnp.float32)

    for side in range(4):
        @pl.when(jnp.logical_not(there[side]))
        def _():
            def clear(slot, carry):
                if side < 2:
                    field[slot, :, side * (ext_x + 1)] = jnp.zeros((shots, ext_y, depth), jnp.float32)
                else:
                    yrecv[slot, side - 2] = jnp.zeros((shots, ext_x, 1, depth), jnp.float32)
                return carry
            lax.fori_loop(1, STEPS + 1, clear, 0)

    def copy(slot, side):
        if side < 2:
            src = field.at[slot, :, 1 if side == 0 else ext_x]
            dst = field.at[slot, :, ext_x + 1 if side == 0 else 0]
        else:
            src = ysend.at[slot, side - 2]
            dst = yrecv.at[slot, 3 - side]
        return pltpu.make_async_remote_copy(
            src_ref=src, dst_ref=dst,
            send_sem=send_sem.at[slot, side], recv_sem=recv_sem.at[slot, side ^ 1],
            device_id=target[side], device_id_type=pl.DeviceIdType.MESH,
        )

    def landing(slot, side):
        if side < 2:
            dst = field.at[slot, :, 0 if side == 0 else ext_x + 1]
        else:
            dst = yrecv.at[slot, side - 2]
        return pltpu.make_async_remote_copy(
            src_ref=dst, dst_ref=dst,
            send_sem=send_sem.at[slot, side], recv_sem=recv_sem.at[slot, side],
            device_id=target[side], device_id_type=pl.DeviceIdType.MESH,
        )

    def send(slot):
        for side in (2, 3, 0, 1):
            @pl.when(there[side])
            def _():
                copy(slot, side).start()

    for load in loads[1:]:
        load.wait()
    ysend[1, 0] = field[1, :, 1 : ext_x + 1, 0:1, :]
    ysend[1, 1] = field[1, :, 1 : ext_x + 1, ext_y - 1 : ext_y, :]
    pl.semaphore_wait(barrier, n_tx - 1 + len(offsets))
    send(1)
    for di in range(1, n_shot):
        share(hist_all, hist_send, hist_recv, di).start()

    cells = ridx_ref[...]
    points = cells.shape[1]
    rows = lax.broadcasted_iota(jnp.int32, (ext_x * ext_y, points), 0)
    pick_xy[...] = jnp.where(rows == cells // depth, 1.0, 0.0).astype(jnp.bfloat16)
    deep = lax.broadcasted_iota(jnp.int32, (depth, points), 0)
    pick_z[...] = jnp.where(deep == cells % depth, 1.0, 0.0)

    loads[0].wait()

    part = 4 if ext_x % 4 == 0 else 1
    shape = (part, ext_y, depth)
    at_y = lax.broadcasted_iota(jnp.int32, shape, 1)
    at_z = lax.broadcasted_iota(jnp.int32, shape, 2)

    def inner(slot):
        def one_shot(s, carry):
            for x0 in range(0, ext_x, part):
                centre = field[slot, s, x0 + 1 : x0 + 1 + part]
                if x0 == 0:
                    below = [jnp.zeros((1, ext_y, depth), jnp.float32)]
                    if part > 1:
                        below.append(field[slot, s, 1:part])
                    below = jnp.concatenate(below, 0)
                else:
                    below = field[slot, s, x0 : x0 + part]
                if x0 + part == ext_x:
                    above = [jnp.zeros((1, ext_y, depth), jnp.float32)]
                    if part > 1:
                        above.insert(0, field[slot, s, x0 + 2 : ext_x + 1])
                    above = jnp.concatenate(above, 0)
                else:
                    above = field[slot, s, x0 + 2 : x0 + 2 + part]
                total = below + above
                total += jnp.where(at_y == 0, 0.0, pltpu.roll(centre, 1, 1))
                total += jnp.where(at_y == ext_y - 1, 0.0, pltpu.roll(centre, ext_y - 1, 1))
                total += jnp.where(at_z == 0, 0.0, pltpu.roll(centre, 1, 2))
                total += jnp.where(at_z == depth - 1, 0.0, pltpu.roll(centre, depth - 1, 2))
                before = field[slot - 1, s, x0 + 1 : x0 + 1 + part]
                speed = cour_ref[x0 : x0 + part]
                field[slot + 1, s, x0 + 1 : x0 + 1 + part] = (
                    2.0 * centre - before + speed * (total - 6.0 * centre)
                )
            return carry
        lax.fori_loop(0, shots, one_shot, 0)

    def border(slot, pack):
        for side in range(2):
            arrive(slot, side)
            halo, edge = (0, 1) if side == 0 else (ext_x + 1, ext_x)
            field[slot + 1, :, edge] += cour_ref[edge - 1][None] * field[slot, :, halo]
        for side in range(2, 4):
            arrive(slot, side)
            edge = 0 if side == 2 else ext_y - 1
            speed = cour_ref[:, edge : edge + 1, :]
            for s in range(shots):
                row = field[slot + 1, s, 1 : ext_x + 1, edge : edge + 1, :]
                row += speed * yrecv[slot, side - 2, s]
                if pack:
                    ysend[slot + 1, side - 2, s] = row
                field[slot + 1, s, 1 : ext_x + 1, edge : edge + 1, :] = row

    def sample(slot):
        for s in range(shots):
            tile = field[slot, s, 1 : ext_x + 1].reshape(ext_x * ext_y, depth).astype(jnp.bfloat16)
            found = lax.dot_general(
                tile, pick_xy[...], (((0,), (0,)), ((), ())), preferred_element_type=jnp.float32
            )
            rec[pl.ds(s * STEPS + slot - 2, 1), :] = jnp.sum(
                found * pick_z[...], axis=0, keepdims=True
            )

    def arrive(slot, side):
        @pl.when(there[side])
        def _():
            landing(slot, side).wait_recv()

    first_early = 2

    def early_part(m):
        early[m] = jnp.dot(
            hist_all[...].reshape(n_shot * rows_each, points), blocks[group_a, m],
            preferred_element_type=jnp.float32,
        )

    def step(slot, carry):
        border(slot, True)
        send(slot + 1)
        sample(slot + 1)
        inner(slot + 1)

        @pl.when(slot == first_early)
        def _():
            for load in green_loads:
                load.wait()
            for di in range(1, n_shot):
                share(hist_all, hist_send, hist_recv, di).wait()

        @pl.when(jnp.logical_and(slot >= first_early, slot < first_early + n_tx))
        def _():
            early_part(slot - first_early)
        return carry

    inner(1)
    lax.fori_loop(1, STEPS, step, 0)
    for m in range(STEPS - first_early, n_tx):
        early_part(m)

    rec_all[0] = rec[...].astype(jnp.bfloat16)
    for di in range(1, n_shot):
        share(rec_all, rec_send, rec_recv, di).start()
    border(STEPS, False)
    stores = [
        pltpu.make_async_copy(field.at[STEPS, :, pl.ds(1, ext_x)], last_ref, load_sem.at[0]),
        pltpu.make_async_copy(field.at[STEPS + 1, :, pl.ds(1, ext_x)], out_ref, load_sem.at[1]),
    ]
    for store in stores:
        store.start()
    for di in range(1, n_shot):
        share(rec_all, rec_send, rec_recv, di).wait()

    to_row = lax.broadcasted_iota(jnp.int32, (rows_each, rows_each), 0)
    of_row = lax.broadcasted_iota(jnp.int32, (rows_each, rows_each), 1)
    same = to_row // STEPS == of_row // STEPS
    wanted = to_row % STEPS - short
    pick_old = jnp.where(same & (of_row % STEPS == wanted + HIST), 1.0, 0.0).astype(jnp.bfloat16)
    pick_new = jnp.where(same & (of_row % STEPS == wanted), 1.0, 0.0).astype(jnp.bfloat16)
    windows = []
    for di in range(n_shot):
        window = jnp.dot(pick_old, hist_all[di], preferred_element_type=jnp.float32)
        window += jnp.dot(pick_new, rec_all[di], preferred_element_type=jnp.float32)
        windows.append(window.astype(jnp.bfloat16))
    window = jnp.concatenate(windows, 0)

    def hand_on(m):
        bit = low_bit(m)
        return pltpu.make_async_remote_copy(
            src_ref=xpart.at[m], dst_ref=xrecv.at[m],
            send_sem=x_send.at[m], recv_sem=x_recv.at[m],
            device_id={"tx": flip(tx, bit)}, device_id_type=mesh_id,
        )

    for m in range(n_tx - 1, -1, -1):
        part = early[m] + jnp.dot(window, blocks[group_b, m], preferred_element_type=jnp.float32)
        for di in range(n_shot):
            xpart[m, (me - di + n_shot) % n_shot] = part[di * rows_each : (di + 1) * rows_each]
        bit = 1
        while bit < (low_bit(m) if m else n_tx):
            hand_on(m + bit).wait_recv()
            xpart[m] += xrecv[m + bit]
            bit *= 2
        if m:
            hand_on(m).start()

    for b in range(n_ty):
        for i in range(n_shot):
            tile = xpart[0, i, :, b * each : (b + 1) * each]
            zpart[b, i] = tile
            zsend[b, i] = tile.astype(jnp.bfloat16)

    def deliver(far, di):
        shot_to, ty_to = place(far, di)
        return pltpu.make_async_remote_copy(
            src_ref=zsend.at[ty_to, shot_to], dst_ref=zrecv.at[far, di],
            send_sem=z_send.at[far, di], recv_sem=z_recv.at[far, di],
            device_id={"shot": shot_to, "ty": ty_to}, device_id_type=mesh_id,
        )

    for far, di in reversed(offsets):
        deliver(far, di).start()

    def drain(slot, carry):
        for side in range(4):
            @pl.when(there[side])
            def _():
                copy(slot, side).wait_send()
        return carry
    lax.fori_loop(1, STEPS + 1, drain, 0)
    for m in range(1, n_tx):
        hand_on(m).wait_send()

    for di in range(n_shot):
        if di == 0:
            total = zpart[ty, me]
        else:
            deliver(0, di).wait()
            total = zrecv[0, di].astype(jnp.float32)
        for far in range(1, n_ty):
            deliver(far, di).wait()
            total += zrecv[far, di].astype(jnp.float32)
        em_ref[(me - di + n_shot) % n_shot] = total
    for store in stores:
        store.wait()


def run_block(n_shot, n_tx, n_ty, lag_delay, wave_now, wave_prev, courant, ridx, history, green):
    shots, ext_x, ext_y, depth = wave_now.shape
    points = ridx.shape[1]
    groups = green.shape[0]
    rows_each = history.shape[0]
    span = green.shape[2] // n_tx
    each = span // n_ty
    if span % 128:
        green = green.reshape(groups, points, n_tx, span).transpose(0, 2, 1, 3)
    whole = pl.BlockSpec(memory_space=pltpu.VMEM)
    far = pl.BlockSpec(memory_space=pl.ANY)
    dma = pltpu.SemaphoreType.DMA
    return pl.pallas_call(
        functools.partial(block_kernel, n_shot, n_tx, n_ty),
        out_shape=(
            jax.ShapeDtypeStruct(wave_now.shape, jnp.float32),
            jax.ShapeDtypeStruct(wave_now.shape, jnp.float32),
            jax.ShapeDtypeStruct((n_shot, rows_each, each), jnp.float32),
        ),
        in_specs=[
            pl.BlockSpec(memory_space=pltpu.SMEM)
        ] + [pl.BlockSpec(memory_space=pltpu.HBM)] * 6,
        out_specs=(far, far, whole),
        scratch_shapes=[
            pltpu.VMEM((ext_x, ext_y, depth), jnp.float32),
            pltpu.VMEM((1, points), jnp.int32),
            pltpu.VMEM((STEPS + 2, shots, ext_x + 2, ext_y, depth), jnp.float32),
            pltpu.VMEM((STEPS + 1, 2, shots, ext_x, 1, depth), jnp.float32),
            pltpu.VMEM((STEPS + 1, 2, shots, ext_x, 1, depth), jnp.float32),
            pltpu.VMEM((ext_x * ext_y, points), jnp.bfloat16),
            pltpu.VMEM((depth, points), jnp.float32),
            pltpu.VMEM((n_shot, rows_each, points), jnp.bfloat16),
            pltpu.VMEM((rows_each, points), jnp.float32),
            pltpu.VMEM((n_shot, rows_each, points), jnp.bfloat16),
            pltpu.VMEM((n_tx, n_shot * rows_each, span), jnp.float32),
            pltpu.VMEM((groups, n_tx, points, span), jnp.bfloat16),
            pltpu.VMEM((n_tx, n_shot, rows_each, span), jnp.float32),
            pltpu.VMEM((n_tx, n_shot, rows_each, span), jnp.float32),
            pltpu.VMEM((n_ty, n_shot, rows_each, each), jnp.float32),
            pltpu.VMEM((n_ty, n_shot, rows_each, each), jnp.bfloat16),
            pltpu.VMEM((n_ty, n_shot, rows_each, each), jnp.bfloat16),
            dma((5,)),
            dma((STEPS + 1, 4)),
            dma((STEPS + 1, 4)),
            dma((groups, n_tx)),
            dma((n_shot,)),
            dma((n_shot,)),
            dma((n_shot,)),
            dma((n_shot,)),
            dma((n_tx,)),
            dma((n_tx,)),
            dma((n_ty, n_shot)),
            dma((n_ty, n_shot)),
        ],
        compiler_params=pltpu.CompilerParams(
            collective_id=0, has_side_effects=True, vmem_limit_bytes=60 * MIB
        ),
    )(lag_delay, wave_now, wave_prev, courant, ridx, history, green)


def inject_kernel(
    previous_ref, wave_far, cells_far, weights_far, columns_far,
    out_ref, last_ref, emission_ref,
    wave_ref, cells_ref, weights_ref, columns_ref, sems, load_sem,
):
    shots, ext_x, ext_y, depth = wave_ref.shape
    n_shot, rows_each, each = columns_ref.shape
    corners = cells_ref.shape[0]
    keep = pltpu.make_async_copy(previous_ref, last_ref, sems.at[shots])
    loads = [
        pltpu.make_async_copy(src, dst, load_sem.at[i])
        for i, (src, dst) in enumerate((
            (columns_far, columns_ref),
            (cells_far, cells_ref),
            (weights_far, weights_ref),
            (wave_far, wave_ref),
        ))
    ]
    for load in loads:
        load.start()
    keep.start()
    for load in loads[:3]:
        load.wait()
    for s in range(shots):
        for t in range(STEPS):
            for i in range(n_shot):
                emission_ref[s, t, 0, :, i * each : (i + 1) * each] = columns_ref[
                    i, s * STEPS + t : s * STEPS + t + 1, :
                ]
    rows = lax.broadcasted_iota(jnp.int32, (ext_x * ext_y, each), 0)
    deep = lax.broadcasted_iota(jnp.int32, (depth, each), 0)
    totals = [jnp.zeros((ext_x * ext_y, depth), jnp.float32) for s in range(shots)]
    for k in range(corners):
        for i in range(n_shot):
            span = slice(i * each, (i + 1) * each)
            cells = cells_ref[k : k + 1, span]
            pick = jnp.where(rows == cells // depth, 1.0, 0.0).astype(jnp.bfloat16)
            here = deep == cells % depth
            for s in range(shots):
                final = (s + 1) * STEPS - 1
                values = weights_ref[k : k + 1, span] * columns_ref[i, final : final + 1, :]
                spread = jnp.where(here, values, 0.0).astype(jnp.bfloat16)
                totals[s] += lax.dot_general(
                    pick, spread, (((1,), (1,)), ((), ())), preferred_element_type=jnp.float32
                )
    stores = []
    loads[3].wait()
    for s in range(shots):
        wave_ref[s] += totals[s].reshape(ext_x, ext_y, depth)
        stores.append(pltpu.make_async_copy(wave_ref.at[s], out_ref.at[s], sems.at[s]))
        stores[-1].start()
    for store in stores + [keep]:
        store.wait()


def inject(previous, wave, cells, weights, columns):
    whole = pl.BlockSpec(memory_space=pltpu.VMEM)
    far = pl.BlockSpec(memory_space=pl.ANY)
    shots = wave.shape[0]
    points = cells.shape[1]
    return pl.pallas_call(
        inject_kernel,
        out_shape=(
            jax.ShapeDtypeStruct(wave.shape, jnp.float32),
            jax.ShapeDtypeStruct(wave.shape, jnp.float32),
            jax.ShapeDtypeStruct((shots, STEPS, 1, 1, points), jnp.float32),
        ),
        in_specs=[pl.BlockSpec(memory_space=pltpu.HBM)] * 5,
        out_specs=(far, far, whole),
        scratch_shapes=[
            pltpu.VMEM(wave.shape, jnp.float32),
            pltpu.VMEM(cells.shape, jnp.int32),
            pltpu.VMEM(weights.shape, jnp.float32),
            pltpu.VMEM(columns.shape, jnp.float32),
            pltpu.SemaphoreType.DMA((shots + 1,)),
            pltpu.SemaphoreType.DMA((4,)),
        ],
        compiler_params=pltpu.CompilerParams(vmem_limit_bytes=60 * MIB),
    )(previous, wave, cells, weights, columns)


def local(
    n_shot, n_tx, n_ty,
    wave_now, wave_prev, courant, rec_index, rec_history, green, lag_delay, emit_cells, emit_weights
):
    shots_here = wave_now.shape[0]
    previous, current, columns = run_block(
        n_shot, n_tx, n_ty, lag_delay, wave_now, wave_prev, courant,
        rec_index.reshape(1, -1), rec_history.reshape(shots_here * HIST, -1), green,
    )
    return inject(
        previous,
        current,
        emit_cells.reshape(emit_cells.shape[-2:]),
        emit_weights.reshape(emit_weights.shape[-2:]),
        columns,
    )


def solution(mesh):
    return jax.shard_map(
        functools.partial(local, mesh.shape["shot"], mesh.shape["tx"], mesh.shape["ty"]),
        mesh=mesh,
        in_specs=(
            P("shot", "tx", "ty", None),
            P("shot", "tx", "ty", None),
            P("tx", "ty", None),
            P("tx", "ty", None),
            P("shot", None, "tx", "ty", None),
            P(None, ("tx", "ty"), "shot"),
            P(),
            P("tx", "ty", None, None),
            P("tx", "ty", None, None),
        ),
        out_specs=(
            P("shot", "tx", "ty", None),
            P("shot", "tx", "ty", None),
            P("shot", None, "tx", "ty", None),
        ),
        check_vma=False,
    )
```
